256 devices in a mesh: dp: 32 (over z_hi, y, core), tensor: 8 (over z_lo, x).
Axes of the slice: x: 4, y: 4, z: 8 (z_hi: 4, z_lo: 2; z = z_hi * 2 + z_lo), core: 2. Of those that a mesh axis runs over, the one named last changes fastest.
Arguments:
- activations: bfloat16 [4096, 8192], P('dp', 'tensor'), may hold values from -12 to 12
- hidden_grad: bfloat16 [4096, 14336], P('dp', 'tensor'), may hold values from -0.049804688 to 0.049804688
- master: float32 [8192, 14336], P('dp', 'tensor'), may hold values from -400 to 400
- moment_one: float32 [8192, 14336], P('dp', 'tensor'), may hold values from -100 to 100
- moment_two: float32 [8192, 14336], P('dp', 'tensor'), may hold values from 0.0001 to 0.01
Outputs:
- input_grad: bfloat16 [4096, 8192], P(('dp', 'tensor'))
- update: float32 [8192, 14336], P('dp', 'tensor')
- new_one: float32 [8192, 14336], P('dp', 'tensor')
- new_two: float32 [8192, 14336], P('dp', 'tensor')
The draws below stay inside these ranges and needn't reach their ends.
All inputs are finite; a program needn't handle non-finite values.
Results may differ from the reference program's by a relative error of at most 0.0049.
Values may be sent and summed in bfloat16 or wider, within the bound.
No kernel may reach another device: no remote copies, remote signals or barrier semaphores. Data moves between devices by JAX's collectives and lax.ppermute only.
A program may use at most 128 MiB of HBM per device.

```python
import math
import jax
import jax.numpy as jnp

D = 8192
FFW = 14336
TOKENS = 4096


def scales(key, count, rise):
    spread = (jax.random.uniform(key, (count,), jnp.float32) - 0.5) * math.log(10.0)
    slope = jnp.arange(count, dtype=jnp.float32) / count * math.log(rise)
    return jnp.exp(spread + slope)


def shaped(key, noise, rise, base):
    key_rows, key_cols = jax.random.split(key, 2)
    return base * noise * scales(key_rows, D, rise)[:, None] * scales(key_cols, FFW, rise)[None, :]


def draw_master(key, part):
    key = jax.random.fold_in(key, 11)
    key_scale, key_noise = jax.random.split(key, 2)
    noise = jnp.clip(jax.random.normal(key_noise, (D, FFW), jnp.float32), -6.0, 6.0)
    return shaped(key_scale, noise, 3.0, 0.2)


def draw_moment_one(key, part):
    key = jax.random.fold_in(key, 12)
    key_scale, key_noise = jax.random.split(key, 2)
    noise = jnp.clip(jax.random.normal(key_noise, (D, FFW), jnp.float32), -6.0, 6.0)
    return shaped(key_scale, noise, 3.0, 0.05)


def block_scale(rng, extent, cuts, least, high):
    def one(axis_at, shards_of):
        draws = jax.random.uniform(jax.random.fold_in(jax.random.fold_in(rng, 6), axis_at), (shards_of,), jnp.float32, least / len(cuts), high / len(cuts))
        return jnp.repeat(jnp.exp(draws), extent[axis_at] // shards_of).reshape((-1,) + (1,) * (len(extent) - axis_at - 1))

    level = one(*cuts[0])
    for cut in cuts[1:]:
        level = level * one(*cut)
    return level


def centred(key, extent, width, limit, cuts=(), held_as=jnp.bfloat16):
    factor_of = block_scale(key, extent, cuts, -0.22, 0.18) if cuts else 1.0
    drawn = jax.random.normal(key, extent, jnp.float32) * width * factor_of
    return jnp.minimum(jnp.maximum(drawn, -limit), limit).astype(held_as)


def setup_inputs(seed: int = 0) -> dict:
    splits = jax.random.split(jax.random.key(seed), 6)
    activations = centred(splits[0], (TOKENS, D), 2.0, 12.0, ((0, 32), (1, 8)))
    hidden_grad = centred(splits[1], (TOKENS, FFW), 0.0078125, 0.049804688, ((0, 32), (1, 8)))
    master = draw_master(jax.random.fold_in(splits[5], 71), 0)
    moment_one = draw_moment_one(jax.random.fold_in(splits[5], 71), 0)
    moment_two = jnp.clip(jnp.exp(math.log(0.01) - 4.6051702 * jax.random.uniform(splits[4], (D, FFW), jnp.float32) ** block_scale(splits[4], (D, FFW), ((0, 32), (1, 8)), -0.2, 0.2)), 0.0001, 0.01)
    return {"activations": activations, "hidden_grad": hidden_grad, "master": master, "moment_one": moment_one, "moment_two": moment_two}


beta_one = 0.9
beta_two = 0.999
corr_one = 1.0 - 0.9 ** 10
corr_two = 1.0 - 0.999 ** 10
adam_eps = 1e-06
decay = 0.01

def reference(activations, hidden_grad, master, moment_one, moment_two):
    weight = master.astype(jnp.bfloat16)
    grad = jnp.dot(activations.T, hidden_grad, preferred_element_type=jnp.float32)
    input_grad = jnp.dot(hidden_grad, weight.T, preferred_element_type=jnp.float32).astype(jnp.bfloat16)
    new_one = beta_one * moment_one + (1.0 - beta_one) * grad
    new_two = beta_two * moment_two + (1.0 - beta_two) * grad * grad
    direction = new_one / corr_one / (jnp.sqrt(new_two / corr_two) + adam_eps) + decay * master
    weight_sq = jnp.sum(master * master)
    direction_sq = jnp.sum(direction * direction)
    trust = jnp.sqrt(weight_sq) / (jnp.sqrt(direction_sq) + adam_eps)
    return (input_grad, trust * direction, new_one, new_two)
```

```python
import jax
import jax.numpy as jnp
from jax import lax
from jax.sharding import Mesh, PartitionSpec as P

beta_one = 0.9
beta_two = 0.999
corr_one = 1.0 - 0.9**10
corr_two = 1.0 - 0.999**10
adam_eps = 1e-06
decay = 0.01

DP = ("zh", "y", "c")
TP = ("zl", "x")
CH = ("zh", "y")
BF = jnp.bfloat16
F32 = jnp.float32


def shift(value, axis, by, size=4):
    return lax.ppermute(value, axis, [(i, (i - by) % size) for i in range(size)])


def ring(block, axis):
    half = block.shape[0] // 2
    one, three = shift(block, axis, 1), shift(block, axis, 3)
    two_low = shift(one[:half], axis, 1)
    two_high = shift(three[half:], axis, 3)
    return [block, one, two_low, two_high, three]


def rolled(value, axis, by):
    return lax.dynamic_slice_in_dim(jnp.concatenate([value, value], axis), by, 4, axis)


def dot(a, b, da, db):
    return lax.dot_general(a, b, (((da,), (db,)), ((), ())), preferred_element_type=F32)


def total(value):
    value = value + shift(value, "c", 1, 2)
    value = value + shift(value, "zl", 1, 2)
    for axis in ("x", "y", "zh"):
        value = value + lax.ppermute(value, axis, [(0, 1), (1, 0), (2, 3), (3, 2)])
        value = value + lax.ppermute(value, axis, [(0, 3), (1, 2), (2, 1), (3, 0)])
    return value


def on_device(activations, hidden_grad, master, moment_one, moment_two):
    zh, y, c = (lax.axis_index(n) for n in DP)
    zl, x = (lax.axis_index(n) for n in TP)

    near, far_low, far_high, back = ring(hidden_grad, "zh")[1:]
    far = jnp.concatenate([far_low, far_high], 0)
    chunks = [jnp.concatenate(ring(b, "y"), 0) for b in (hidden_grad, near, far, back)]

    rows = lax.all_to_all(activations, TP, split_axis=0, concat_axis=1, tiled=True)
    rows = lax.all_to_all(rows, CH, split_axis=1, concat_axis=0, tiled=True)
    rows = rows.reshape(4, 4, 16, 512)
    rows = rolled(rolled(rows, 0, zh), 1, y)
    feats = lax.all_gather(rows, TP, axis=2, tiled=True)
    feats = feats.reshape(4, 512, 2, 256)
    mine_a = lax.dynamic_index_in_dim(feats, c, 2, keepdims=False)
    other_a = lax.dynamic_index_in_dim(feats, 1 - c, 2, keepdims=False)

    weight = master.astype(BF)
    weight_other = shift(weight, "c", 1, 2)
    both = jnp.where(
        c == 0,
        jnp.concatenate([weight, weight_other], 0),
        jnp.concatenate([weight_other, weight], 0),
    )

    parts = []
    for chunk in chunks:
        part = dot(chunk, both, 1, 1).astype(BF).reshape(4, 2, 4, 16, 512)
        pick = lambda k: lax.dynamic_index_in_dim(part, (x + k) % 4, 2, keepdims=False)
        acc = pick(0).astype(F32)
        for k in (1, 3, 2):
            acc = acc + shift(pick(k), "x", 4 - k).astype(F32)
        mine = lax.dynamic_index_in_dim(acc, zl, 1, keepdims=False)
        other = lax.dynamic_index_in_dim(acc, 1 - zl, 1, keepdims=False).astype(BF)
        mine = mine + shift(other, "zl", 1, 2).astype(F32)
        parts.append(mine.astype(BF))
    out = jnp.stack(parts, 0)
    out = rolled(rolled(out, 0, (4 - zh) % 4), 1, (4 - y) % 4)
    out = lax.all_to_all(out.reshape(16, 16, 512), CH, split_axis=0, concat_axis=0, tiled=True)
    input_grad = out.transpose(1, 0, 2).reshape(16, 8192)

    grad_other = sum(dot(other_a[i], chunks[i], 0, 0) for i in range(4))
    grad = sum(dot(mine_a[i], chunks[i], 0, 0) for i in range(4))
    grad = grad + shift(grad_other, "c", 1, 2)

    new_one = beta_one * moment_one + (1.0 - beta_one) * grad
    new_two = beta_two * moment_two + (1.0 - beta_two) * grad * grad
    direction = new_one / corr_one / (jnp.sqrt(new_two / corr_two) + adam_eps) + decay * master
    sums = total(jnp.stack([jnp.sum(master * master), jnp.sum(direction * direction)]))
    trust = jnp.sqrt(sums[0]) / (jnp.sqrt(sums[1]) + adam_eps)
    return (input_grad, trust * direction, new_one, new_two)


def solution(mesh):
    fine = Mesh(mesh.devices.reshape(4, 4, 2, 2, 4), DP + TP)
    return jax.shard_map(
        on_device,
        mesh=fine,
        in_specs=(P(DP, TP),) * 5,
        out_specs=(P(DP + TP, None), P(DP, TP), P(DP, TP), P(DP, TP)),
        check_vma=False,
    )
```

```python
import jax
import jax.numpy as jnp
from jax import lax
from jax.experimental import pallas as pl
from jax.experimental.pallas import tpu as pltpu
from jax.sharding import Mesh, PartitionSpec as P

beta_one = 0.9
beta_two = 0.999
corr_one = 1.0 - 0.9**10
corr_two = 1.0 - 0.999**10
adam_eps = 1e-06
decay = 0.01

DP = ("zh", "y", "c")
TP = ("zl", "x")
CH = ("zh", "y")
BF = jnp.bfloat16
F32 = jnp.float32


def shift(value, axis, by, size=4):
    return lax.ppermute(value, axis, [(i, (i - by) % size) for i in range(size)])


def ends(value, axis):
    return shift(value, axis, 1), shift(value, axis, 3)


def middle(one, three, axis):
    half = one.shape[0] // 2
    return shift(one[:half], axis, 1), shift(three[half:], axis, 3)


def rolled(value, axis, by):
    return lax.dynamic_slice_in_dim(jnp.concatenate([value, value], axis), by, 4, axis)


def dot(a, b, da, db):
    return lax.dot_general(a, b, (((da,), (db,)), ((), ())), preferred_element_type=F32)


def thirds(value):
    one = lax.reduce_precision(value, 8, 7)
    two = lax.reduce_precision(value - one, 8, 7)
    three = lax.reduce_precision(value - one - two, 8, 7)
    return jnp.concatenate([one, two, three]).astype(BF)


sync = lambda *values: lax.optimization_barrier(values)
cat = lambda *values: jnp.concatenate(values, 0)


def params(limit=56):
    return pltpu.CompilerParams(dimension_semantics=("arbitrary",), vmem_limit_bytes=limit << 20)


def fetch(pieces, tokens_ref, sems):
    copies, at = [], 0
    for i, piece in enumerate(pieces):
        size = piece.shape[0]
        copies.append(pltpu.make_async_copy(piece, tokens_ref.at[pl.ds(at, size)], sems.at[i]))
        copies[-1].start()
        at += size
    return copies


def part_kernel(*refs):
    pieces, (weight_ref, part_ref, tokens_ref, sems) = refs[:6], refs[6:]
    copies = fetch(pieces, tokens_ref, sems)
    for half in range(2):
        for copy in copies[1:] if half else copies[:1]:
            copy.wait()
        part = dot(tokens_ref[1024 * half : 1024 * half + 1024], weight_ref[...], 1, 1)
        part_ref[:, 16 * half : 16 * half + 16] = part.reshape(16, 8, 8, 512).swapaxes(0, 1).astype(BF)


def grad_kernel(*refs):
    pieces, (feats_ref, grad_ref, grad_other_ref, tokens_ref, sems) = refs[:6], refs[6:]
    for copy in fetch(pieces, tokens_ref, sems):
        copy.wait()
    grad = dot(feats_ref[...], tokens_ref[...], 1, 0)
    grad_ref[...] = grad[:256]
    grad_other_ref[...] = grad[256:]


def place_kernel(places_ref, got_ref, out_ref):
    for i in range(16):
        out_ref[places_ref[i], :8] = jnp.sum(got_ref[:, 16 + i].astype(F32), 0)
        out_ref[i, 8:] = jnp.sum(got_ref[:, i].astype(F32), 0)


def last_kernel(
    grad_ref, other_ref, one_ref, two_ref, master_ref, new_one_ref, new_two_ref, direction_ref, sums_ref, acc_ref
):
    step = pl.program_id(0)

    @pl.when(step == 0)
    def _():
        acc_ref[...] = jnp.zeros_like(acc_ref)

    grad = grad_ref[...] + other_ref[...]
    master = master_ref[...]
    new_one = beta_one * one_ref[...] + (1.0 - beta_one) * grad
    new_two = beta_two * two_ref[...] + (1.0 - beta_two) * grad * grad
    direction = new_one / corr_one / (jnp.sqrt(new_two / corr_two) + adam_eps) + decay * master
    new_one_ref[...] = new_one
    new_two_ref[...] = new_two
    direction_ref[...] = direction
    fold = lambda value: jnp.sum((value * value).reshape(-1, 8, 1792), 0)
    acc_ref[0] += fold(master)
    acc_ref[1] += fold(direction)

    @pl.when(step == pl.num_programs(0) - 1)
    def _():
        lane = lax.broadcasted_iota(jnp.int32, sums_ref.shape, 1)
        sums_ref[...] = jnp.where(
            lane == 0, jnp.sum(acc_ref[0]), jnp.where(lane == 1, jnp.sum(acc_ref[1]), 0.0)
        )


def whole(*shape):
    return pl.BlockSpec(shape, lambda i: (0,) * len(shape))


def cost(flops, size):
    return pl.CostEstimate(flops=flops, bytes_accessed=size, transcendentals=0)


def on_device(activations, hidden_grad, master, moment_one, moment_two):
    zh, y, c = (lax.axis_index(n) for n in DP)
    f32 = jax.ShapeDtypeStruct((256, 1792), F32)

    halves = hidden_grad.reshape(8, 2, 8, 1792)
    second = lax.all_gather(halves[:, 1].reshape(64, 1792), CH, axis=0, tiled=True)
    mine = halves[:, 0].reshape(64, 1792)

    z1, z3 = ends(mine, "zh")
    rows = lax.all_to_all(activations, TP, split_axis=0, concat_axis=1, tiled=True)
    z1, z3, rows, master_late = sync(z1, z3, rows, master)
    z2 = middle(z1, z3, "zh")
    rows = lax.all_to_all(rows, CH, split_axis=1, concat_axis=0, tiled=True)
    *z2, rows = sync(*z2, rows)

    y0 = cat(mine, z1, *z2, z3)
    y1, y3 = ends(y0, "y")
    rows = lax.dynamic_slice_in_dim(jnp.concatenate([rows, rows[:, :256]], 1), 256 * c, 512, 1)
    rows = rows.reshape(4, 4, 2, 8, 512).transpose(2, 1, 0, 3, 4)
    rows = jnp.stack([rows[1].swapaxes(0, 1), rolled(rolled(rows[0], 0, y), 1, zh)])
    copies = jnp.broadcast_to(rows.reshape(1, 2, 16, 8, 512), (8, 2, 16, 8, 512))
    feats = lax.all_to_all(copies, TP, split_axis=0, concat_axis=0, tiled=True)
    y1, y3, _ = sync(y1, y3, copies)
    *y2, second = sync(*middle(y1, y3, "y"), second)

    weight = master_late.astype(BF)
    weight_other = shift(weight, "c", 1, 2)
    both = jnp.where(c == 0, cat(weight, weight_other), cat(weight_other, weight))
    both, second = sync(both, second)

    feats = feats.transpose(4, 1, 2, 0, 3).reshape(512, 2048)
    *y2, both, feats, y0, y1, y3, second = sync(*y2, both, feats, y0, y1, y3, second)

    vmem, anywhere = (pl.BlockSpec(memory_space=space) for space in (pltpu.VMEM, pl.ANY))
    pieces = (second, y0, y1, *y2, y3)
    scratch = [pltpu.VMEM((2048, 1792), BF), pltpu.SemaphoreType.DMA((6,))]
    limit = pltpu.CompilerParams(vmem_limit_bytes=48 << 20)
    part = pl.pallas_call(
        part_kernel,
        in_specs=[anywhere] * 6 + [vmem],
        out_specs=vmem,
        out_shape=jax.ShapeDtypeStruct((8, 32, 8, 512), BF),
        scratch_shapes=scratch,
        compiler_params=limit,
        cost_estimate=cost(2 * 2048 * 512 * 1792, 12 << 20),
    )(*pieces, both)
    got = lax.all_to_all(part, TP, split_axis=0, concat_axis=0, tiled=True)
    feats, _ = sync(feats, part)
    grad, grad_other = pl.pallas_call(
        grad_kernel,
        in_specs=[anywhere] * 6 + [vmem],
        out_specs=[vmem] * 2,
        out_shape=[f32] * 2,
        scratch_shapes=scratch,
        compiler_params=limit,
        cost_estimate=cost(2 * 2048 * 512 * 1792, 12 << 20),
    )(*pieces, feats)
    grad_other = shift(grad_other, "c", 1, 2)
    places = jnp.stack([4 * ((zh + z) % 4) + (y + k) % 4 for k in range(4) for z in range(4)])
    out = pl.pallas_call(
        place_kernel,
        out_shape=jax.ShapeDtypeStruct((16, 16, 512), F32),
        in_specs=[pl.BlockSpec(memory_space=pltpu.SMEM)] + [pl.BlockSpec(memory_space=pltpu.VMEM)],
        compiler_params=pltpu.CompilerParams(vmem_limit_bytes=8 << 20),
        cost_estimate=cost(0, 2 << 20),
    )(places.astype(jnp.int32), got)
    slab = pl.BlockSpec((64, 1792), lambda i: (i, 0))
    new_one, new_two, direction, sums = pl.pallas_call(
        last_kernel,
        grid=(4,),
        in_specs=[slab] * 5,
        out_specs=[slab] * 3 + [whole(16, 128)],
        out_shape=[f32] * 3 + [jax.ShapeDtypeStruct((16, 128), F32)],
        scratch_shapes=[pltpu.VMEM((2, 8, 1792), F32)],
        compiler_params=params(),
        cost_estimate=cost(0, 8 << 20),
    )(grad, grad_other, moment_one, moment_two, master)
    sums, out = sync(sums, out)
    sums = jnp.sum(lax.all_to_all(sums, ("c",) + TP, split_axis=0, concat_axis=0, tiled=True), 0)[:2]

    extra = jnp.broadcast_to(jnp.pad(thirds(sums), (0, 506)), (16, 8, 512))
    out = jnp.concatenate([out.astype(BF), extra], 1)
    out = lax.all_to_all(out, CH, split_axis=0, concat_axis=0, tiled=True)
    input_grad = out[:, :16].transpose(1, 0, 2).reshape(16, 8192)
    sums = jnp.sum(out[:, 16, :6].astype(F32).reshape(16, 3, 2), (0, 1))
    trust = jnp.sqrt(sums[0]) / (jnp.sqrt(sums[1]) + adam_eps)
    return (input_grad, trust * direction, new_one, new_two)


def solution(mesh):
    fine = Mesh(mesh.devices.reshape(4, 4, 2, 2, 4), DP + TP)
    return jax.shard_map(
        on_device,
        mesh=fine,
        in_specs=(P(DP, TP),) * 5,
        out_specs=(P(DP + TP, None), P(DP, TP), P(DP, TP), P(DP, TP)),
        check_vma=False,
    )
```

```python
import jax
import jax.numpy as jnp
from jax import lax
from jax.experimental import pallas as pl
from jax.experimental.pallas import tpu as pltpu
from jax.sharding import Mesh, PartitionSpec as P

beta_one = 0.9
beta_two = 0.999
corr_one = 1.0 - 0.9**10
corr_two = 1.0 - 0.999**10
adam_eps = 1e-06
decay = 0.01

DP = ("zh", "y", "c")
TP = ("zl", "x")
CH = ("zh", "y")
BF = jnp.bfloat16
F32 = jnp.float32


def shift(value, axis, by, size=4):
    return lax.ppermute(value, axis, [(i, (i - by) % size) for i in range(size)])


def ends(value, axis):
    return shift(value, axis, 1), shift(value, axis, 3)


def middle(one, three, axis):
    half = one.shape[0] // 2
    return shift(one[:half], axis, 1), shift(three[half:], axis, 3)


def rolled(value, axis, by):
    return lax.dynamic_slice_in_dim(jnp.concatenate([value, value], axis), by, 4, axis)


def dot(a, b, da, db):
    return lax.dot_general(a, b, (((da,), (db,)), ((), ())), preferred_element_type=F32)


def thirds(value):
    one = lax.reduce_precision(value, 8, 7)
    two = lax.reduce_precision(value - one, 8, 7)
    three = lax.reduce_precision(value - one - two, 8, 7)
    return jnp.concatenate([one, two, three]).astype(BF)


sync = lambda *values: lax.optimization_barrier(values)
cat = lambda *values: jnp.concatenate(values, 0)


def params(limit=60):
    return pltpu.CompilerParams(dimension_semantics=("arbitrary",), vmem_limit_bytes=limit << 20)


def fetch(pieces, tokens_ref, sems):
    copies, at = [], 0
    for i, piece in enumerate(pieces):
        size = piece.shape[0]
        copies.append(pltpu.make_async_copy(piece, tokens_ref.at[pl.ds(at, size)], sems.at[i]))
        copies[-1].start()
        at += size
    return copies


def part_kernel(*refs):
    pieces, (weight_ref, part_ref, tokens_ref, sems) = refs[:6], refs[6:]
    copies = fetch(pieces, tokens_ref, sems)
    for half in range(2):
        for copy in copies[1:] if half else copies[:1]:
            copy.wait()
        part = dot(tokens_ref[1024 * half : 1024 * half + 1024], weight_ref[...], 1, 1)
        part_ref[:, 16 * half : 16 * half + 16] = part.reshape(16, 8, 8, 512).swapaxes(0, 1).astype(BF)


def grad_kernel(*refs):
    pieces, (feats_ref, grad_ref, grad_other_ref, tokens_ref, sems) = refs[:6], refs[6:]
    copies = fetch(pieces, tokens_ref, sems)
    feats = [feats_ref[:, i].astype(F32).swapaxes(0, 1).reshape(1024, 512).astype(BF) for i in range(2)]
    for copy in copies:
        copy.wait()
    grad = dot(jnp.concatenate(feats, 0), tokens_ref[...], 0, 0)
    grad_ref[...] = grad[:256]
    grad_other_ref[...] = grad[256:]


def place_kernel(places_ref, got_ref, out_ref):
    for i in range(16):
        out_ref[places_ref[i], :8] = jnp.sum(got_ref[:, 16 + i].astype(F32), 0)
        out_ref[i, 8:] = jnp.sum(got_ref[:, i].astype(F32), 0)


def last_kernel(
    grad_ref, other_ref, one_ref, two_ref, master_ref, new_one_ref, new_two_ref, direction_ref, sums_ref, acc_ref
):
    step = pl.program_id(0)

    @pl.when(step == 0)
    def _():
        acc_ref[...] = jnp.zeros_like(acc_ref)

    grad = grad_ref[...] + other_ref[...]
    master = master_ref[...]
    new_one = beta_one * one_ref[...] + (1.0 - beta_one) * grad
    new_two = beta_two * two_ref[...] + (1.0 - beta_two) * grad * grad
    direction = new_one / corr_one / (jnp.sqrt(new_two / corr_two) + adam_eps) + decay * master
    new_one_ref[...] = new_one
    new_two_ref[...] = new_two
    direction_ref[...] = direction
    fold = lambda value: jnp.sum((value * value).reshape(-1, 8, 1792), 0)
    acc_ref[0] += fold(master)
    acc_ref[1] += fold(direction)

    @pl.when(step == pl.num_programs(0) - 1)
    def _():
        lane = lax.broadcasted_iota(jnp.int32, sums_ref.shape, 1)
        sums_ref[...] = jnp.where(
            lane == 0, jnp.sum(acc_ref[0]), jnp.where(lane == 1, jnp.sum(acc_ref[1]), 0.0)
        )


def whole(*shape):
    return pl.BlockSpec(shape, lambda i: (0,) * len(shape))


def cost(flops, size):
    return pl.CostEstimate(flops=flops, bytes_accessed=size, transcendentals=0)


def on_device(activations, hidden_grad, master, moment_one, moment_two):
    zh, y, c = (lax.axis_index(n) for n in DP)
    f32 = jax.ShapeDtypeStruct((256, 1792), F32)

    halves = hidden_grad.reshape(8, 2, 8, 1792)
    second = lax.all_gather(halves[:, 1].reshape(64, 1792), CH, axis=0, tiled=True)
    mine = halves[:, 0].reshape(64, 1792)

    z1, z3 = ends(mine, "zh")
    rows = lax.all_to_all(activations, TP, split_axis=0, concat_axis=1, tiled=True)
    z1, z3, rows, master_late = sync(z1, z3, rows, master)
    z2 = middle(z1, z3, "zh")
    rows = lax.all_to_all(rows, CH, split_axis=1, concat_axis=0, tiled=True)
    *z2, rows = sync(*z2, rows)

    y0 = cat(mine, z1, *z2, z3)
    y1, y3 = ends(y0, "y")
    rows = lax.dynamic_slice_in_dim(jnp.concatenate([rows, rows[:, :256]], 1), 256 * c, 512, 1)
    rows = rows.reshape(4, 4, 2, 8, 512).transpose(2, 1, 0, 3, 4)
    rows = jnp.stack([rows[1].swapaxes(0, 1), rolled(rolled(rows[0], 0, y), 1, zh)])
    copies = jnp.broadcast_to(rows.reshape(1, 2, 16, 8, 512), (8, 2, 16, 8, 512))
    feats = lax.all_to_all(copies, TP, split_axis=0, concat_axis=0, tiled=True)
    *y2, second = sync(*middle(y1, y3, "y"), second)

    weight = master_late.astype(BF)
    weight_other = shift(weight, "c", 1, 2)
    both = jnp.where(c == 0, cat(weight, weight_other), cat(weight_other, weight))
    both, second = sync(both, second)

    *y2, both, y0, y1, y3, second = sync(*y2, both, y0, y1, y3, second)

    vmem, anywhere = (pl.BlockSpec(memory_space=space) for space in (pltpu.VMEM, pltpu.HBM))
    pieces = (second, y0, y1, *y2, y3)
    scratch = [pltpu.VMEM((2048, 1792), BF), pltpu.SemaphoreType.DMA((6,))]
    limit = pltpu.CompilerParams(vmem_limit_bytes=60 << 20)
    part = pl.pallas_call(
        part_kernel,
        in_specs=[anywhere] * 6 + [vmem],
        out_specs=vmem,
        out_shape=jax.ShapeDtypeStruct((8, 32, 8, 512), BF),
        scratch_shapes=scratch,
        compiler_params=limit,
        cost_estimate=cost(2 * 2048 * 512 * 1792, 12 << 20),
    )(*pieces, both)
    got = lax.all_to_all(part, TP, split_axis=0, concat_axis=0, tiled=True)
    feats, _ = sync(feats, part)
    grad, grad_other = pl.pallas_call(
        grad_kernel,
        in_specs=[anywhere] * 6 + [vmem],
        out_specs=[vmem] * 2,
        out_shape=[f32] * 2,
        scratch_shapes=scratch,
        compiler_params=limit,
        cost_estimate=cost(2 * 2048 * 512 * 1792, 12 << 20),
    )(*pieces, feats)
    grad_other = shift(grad_other, "c", 1, 2)
    places = jnp.stack([4 * ((zh + z) % 4) + (y + k) % 4 for k in range(4) for z in range(4)])
    out = pl.pallas_call(
        place_kernel,
        out_shape=jax.ShapeDtypeStruct((16, 16, 512), F32),
        in_specs=[pl.BlockSpec(memory_space=pltpu.SMEM)] + [pl.BlockSpec(memory_space=pltpu.VMEM)],
        compiler_params=pltpu.CompilerParams(vmem_limit_bytes=8 << 20),
        cost_estimate=cost(0, 2 << 20),
    )(places.astype(jnp.int32), got)
    slab = pl.BlockSpec((128, 1792), lambda i: (i, 0))
    new_one, new_two, direction, sums = pl.pallas_call(
        last_kernel,
        grid=(2,),
        in_specs=[slab] * 5,
        out_specs=[slab] * 3 + [whole(16, 128)],
        out_shape=[f32] * 3 + [jax.ShapeDtypeStruct((16, 128), F32)],
        scratch_shapes=[pltpu.VMEM((2, 8, 1792), F32)],
        compiler_params=params(),
        cost_estimate=cost(0, 8 << 20),
    )(grad, grad_other, moment_one, moment_two, master)
    sums, out = sync(sums, out)
    sums = jnp.sum(lax.all_to_all(sums, ("c",) + TP, split_axis=0, concat_axis=0, tiled=True), 0)[:2]

    extra = jnp.broadcast_to(jnp.pad(thirds(sums), (0, 506)), (16, 8, 512))
    out = jnp.concatenate([out.astype(BF), extra], 1)
    out = lax.all_to_all(out, CH, split_axis=0, concat_axis=0, tiled=True)
    input_grad = out[:, :16].transpose(1, 0, 2).reshape(16, 8192)
    sums = jnp.sum(out[:, 16, :6].astype(F32).reshape(16, 3, 2), (0, 1))
    trust = jnp.sqrt(sums[0]) / (jnp.sqrt(sums[1]) + adam_eps)
    return (input_grad, trust * direction, new_one, new_two)


def solution(mesh):
    fine = Mesh(mesh.devices.reshape(4, 4, 2, 2, 4), DP + TP)
    return jax.shard_map(
        on_device,
        mesh=fine,
        in_specs=(P(DP, TP),) * 5,
        out_specs=(P(DP + TP, None), P(DP, TP), P(DP, TP), P(DP, TP)),
        check_vma=False,
    )
```

```python
import jax
import jax.numpy as jnp
from jax import lax
from jax.experimental import pallas as pl
from jax.experimental.pallas import tpu as pltpu
from jax.sharding import Mesh, PartitionSpec as P

beta_one = 0.9
beta_two = 0.999
corr_one = 1.0 - 0.9**10
corr_two = 1.0 - 0.999**10
adam_eps = 1e-06
decay = 0.01

DP = ("zh", "y", "c")
TP = ("zl", "x")
CH = ("zh", "y")
BF = jnp.bfloat16
F32 = jnp.float32


def shift(value, axis, by, size=4):
    return lax.ppermute(value, axis, [(i, (i - by) % size) for i in range(size)])


def ends(value, axis):
    return shift(value, axis, 1), shift(value, axis, 3)


def middle(one, three, axis):
    half = one.shape[0] // 2
    return shift(one[:half], axis, 1), shift(three[half:], axis, 3)


def rolled(value, axis, by):
    return lax.dynamic_slice_in_dim(jnp.concatenate([value, value], axis), by, 4, axis)


def dot(a, b, da, db):
    return lax.dot_general(a, b, (((da,), (db,)), ((), ())), preferred_element_type=F32)


def thirds(value):
    one = lax.reduce_precision(value, 8, 7)
    two = lax.reduce_precision(value - one, 8, 7)
    three = lax.reduce_precision(value - one - two, 8, 7)
    return jnp.concatenate([one, two, three]).astype(BF)


sync = lambda *values: lax.optimization_barrier(values)
cat = lambda *values: jnp.concatenate(values, 0)


def params(limit=60):
    return pltpu.CompilerParams(dimension_semantics=("arbitrary",), vmem_limit_bytes=limit << 20)


def fetch(pieces, tokens_ref, sems):
    copies, at = [], 0
    for i, piece in enumerate(pieces):
        size = piece.shape[0]
        copies.append(pltpu.make_async_copy(piece, tokens_ref.at[pl.ds(at, size)], sems.at[i]))
        copies[-1].start()
        at += size
    return copies


def part_kernel(*refs):
    pieces, (weight_ref, part_ref, tokens_ref, sems) = refs[:6], refs[6:]
    copies = fetch(pieces, tokens_ref, sems)
    for half in range(2):
        for copy in copies[1:] if half else copies[:1]:
            copy.wait()
        part = dot(tokens_ref[1024 * half : 1024 * half + 1024], weight_ref[...], 1, 1)
        part_ref[:, 16 * half : 16 * half + 16] = part.reshape(16, 8, 8, 512).swapaxes(0, 1).astype(BF)


def grad_kernel(*refs):
    pieces, (feats_ref, grad_ref, grad_other_ref, tokens_ref, sems) = refs[:6], refs[6:]
    copies = fetch(pieces, tokens_ref, sems)
    feats = [feats_ref[:, i].astype(F32).swapaxes(0, 1).reshape(1024, 512).astype(BF) for i in range(2)]
    for copy in copies:
        copy.wait()
    grad = dot(jnp.concatenate(feats, 0), tokens_ref[...], 0, 0)
    grad_ref[...] = grad[:256]
    grad_other_ref[...] = grad[256:].astype(BF)


def place_kernel(places_ref, got_ref, out_ref):
    for i in range(16):
        out_ref[places_ref[i], :8] = jnp.sum(got_ref[:, 16 + i].astype(F32), 0)
        out_ref[i, 8:] = jnp.sum(got_ref[:, i].astype(F32), 0)


def last_kernel(
    grad_ref, other_ref, one_ref, two_ref, master_ref, new_one_ref, new_two_ref, direction_ref, sums_ref, acc_ref
):
    step = pl.program_id(0)

    @pl.when(step == 0)
    def _():
        acc_ref[...] = jnp.zeros_like(acc_ref)

    grad = grad_ref[...] + other_ref[...].astype(F32)
    master = master_ref[...]
    new_one = beta_one * one_ref[...] + (1.0 - beta_one) * grad
    new_two = beta_two * two_ref[...] + (1.0 - beta_two) * grad * grad
    direction = new_one / corr_one / (jnp.sqrt(new_two / corr_two) + adam_eps) + decay * master
    new_one_ref[...] = new_one
    new_two_ref[...] = new_two
    direction_ref[...] = direction
    fold = lambda value: jnp.sum((value * value).reshape(-1, 8, 1792), 0)
    acc_ref[0] += fold(master)
    acc_ref[1] += fold(direction)

    @pl.when(step == pl.num_programs(0) - 1)
    def _():
        lane = lax.broadcasted_iota(jnp.int32, sums_ref.shape, 1)
        sums_ref[...] = jnp.where(
            lane == 0, jnp.sum(acc_ref[0]), jnp.where(lane == 1, jnp.sum(acc_ref[1]), 0.0)
        )


def whole(*shape):
    return pl.BlockSpec(shape, lambda i: (0,) * len(shape))


def cost(flops, size):
    return pl.CostEstimate(flops=flops, bytes_accessed=size, transcendentals=0)


def on_device(activations, hidden_grad, master, moment_one, moment_two):
    zh, y, c = (lax.axis_index(n) for n in DP)
    f32 = jax.ShapeDtypeStruct((256, 1792), F32)

    halves = hidden_grad.reshape(8, 2, 8, 1792)
    second = lax.all_gather(halves[:, 1].reshape(64, 1792), CH, axis=0, tiled=True)
    mine = halves[:, 0].reshape(64, 1792)

    z1, z3 = ends(mine, "zh")
    rows = lax.all_to_all(activations, TP, split_axis=0, concat_axis=1, tiled=True)
    z1, z3, rows, master_late = sync(z1, z3, rows, master)
    z2 = middle(z1, z3, "zh")
    rows = lax.all_to_all(rows, CH, split_axis=1, concat_axis=0, tiled=True)
    *z2, rows = sync(*z2, rows)

    y0 = cat(mine, z1, *z2, z3)
    y1, y3 = ends(y0, "y")
    rows = lax.dynamic_slice_in_dim(jnp.concatenate([rows, rows[:, :256]], 1), 256 * c, 512, 1)
    rows = rows.reshape(4, 4, 2, 8, 512).transpose(2, 1, 0, 3, 4)
    rows = jnp.stack([rows[1].swapaxes(0, 1), rolled(rolled(rows[0], 0, y), 1, zh)])
    copies = jnp.broadcast_to(rows.reshape(1, 2, 16, 8, 512), (8, 2, 16, 8, 512))
    feats = lax.all_to_all(copies, TP, split_axis=0, concat_axis=0, tiled=True)
    *y2, second = sync(*middle(y1, y3, "y"), second)

    weight = master_late.astype(BF)
    weight_other = shift(weight, "c", 1, 2)
    both = jnp.where(c == 0, cat(weight, weight_other), cat(weight_other, weight))
    both, second = sync(both, second)

    *y2, both, y0, y1, y3, second = sync(*y2, both, y0, y1, y3, second)

    vmem, anywhere = (pl.BlockSpec(memory_space=space) for space in (pltpu.VMEM, pltpu.HBM))
    pieces = (second, y0, y1, *y2, y3)
    scratch = [pltpu.VMEM((2048, 1792), BF), pltpu.SemaphoreType.DMA((6,))]
    limit = pltpu.CompilerParams(vmem_limit_bytes=60 << 20)
    part = pl.pallas_call(
        part_kernel,
        in_specs=[anywhere] * 6 + [vmem],
        out_specs=vmem,
        out_shape=jax.ShapeDtypeStruct((8, 32, 8, 512), BF),
        scratch_shapes=scratch,
        compiler_params=limit,
        cost_estimate=cost(2 * 2048 * 512 * 1792, 12 << 20),
    )(*pieces, both)
    got = lax.all_to_all(part, TP, split_axis=0, concat_axis=0, tiled=True)
    feats, _ = sync(feats, part)
    grad, grad_other = pl.pallas_call(
        grad_kernel,
        in_specs=[anywhere] * 6 + [vmem],
        out_specs=[vmem] * 2,
        out_shape=[f32, jax.ShapeDtypeStruct((256, 1792), BF)],
        scratch_shapes=scratch,
        compiler_params=limit,
        cost_estimate=cost(2 * 2048 * 512 * 1792, 12 << 20),
    )(*pieces, feats)
    grad_other = shift(grad_other, "c", 1, 2)
    places = jnp.stack([4 * ((zh + z) % 4) + (y + k) % 4 for k in range(4) for z in range(4)])
    out = pl.pallas_call(
        place_kernel,
        out_shape=jax.ShapeDtypeStruct((16, 16, 512), F32),
        in_specs=[pl.BlockSpec(memory_space=pltpu.SMEM)] + [pl.BlockSpec(memory_space=pltpu.VMEM)],
        compiler_params=pltpu.CompilerParams(vmem_limit_bytes=8 << 20),
        cost_estimate=cost(0, 2 << 20),
    )(places.astype(jnp.int32), got)
    slab = pl.BlockSpec((128, 1792), lambda i: (i, 0))
    new_one, new_two, direction, sums = pl.pallas_call(
        last_kernel,
        grid=(2,),
        in_specs=[slab] * 5,
        out_specs=[slab] * 3 + [whole(16, 128)],
        out_shape=[f32] * 3 + [jax.ShapeDtypeStruct((16, 128), F32)],
        scratch_shapes=[pltpu.VMEM((2, 8, 1792), F32)],
        compiler_params=params(),
        cost_estimate=cost(0, 8 << 20),
    )(grad, grad_other, moment_one, moment_two, master)
    sums, out = sync(sums, out)
    sums = jnp.sum(lax.all_to_all(sums, ("c",) + TP, split_axis=0, concat_axis=0, tiled=True), 0)[:2]

    extra = jnp.broadcast_to(jnp.pad(thirds(sums), (0, 506)), (16, 8, 512))
    out = jnp.concatenate([out.astype(BF), extra], 1)
    out = lax.all_to_all(out, CH, split_axis=0, concat_axis=0, tiled=True)
    input_grad = out[:, :16].transpose(1, 0, 2).reshape(16, 8192)
    sums = jnp.sum(out[:, 16, :6].astype(F32).reshape(16, 3, 2), (0, 1))
    trust = jnp.sqrt(sums[0]) / (jnp.sqrt(sums[1]) + adam_eps)
    return (input_grad, trust * direction, new_one, new_two)


def solution(mesh):
    fine = Mesh(mesh.devices.reshape(4, 4, 2, 2, 4), DP + TP)
    return jax.shard_map(
        on_device,
        mesh=fine,
        in_specs=(P(DP, TP),) * 5,
        out_specs=(P(DP + TP, None), P(DP, TP), P(DP, TP), P(DP, TP)),
        check_vma=False,
    )
```

```python
import functools

import jax
import jax.numpy as jnp
from jax import lax
from jax.experimental import pallas as pl
from jax.experimental.pallas import tpu as pltpu
from jax.sharding import Mesh, PartitionSpec as P

beta_one = 0.9
beta_two = 0.999
corr_one = 1.0 - 0.9**10
corr_two = 1.0 - 0.999**10
adam_eps = 1e-06
decay = 0.01

DP = ("zh", "y", "c")
TP = ("zl", "x")
CH = ("zh", "y")
BF = jnp.bfloat16
F32 = jnp.float32


def shift(value, axis, by, size=4):
    return lax.ppermute(value, axis, [(i, (i - by) % size) for i in range(size)])


def ends(value, axis):
    return shift(value, axis, 1), shift(value, axis, 3)


def middle(one, three, axis):
    half = one.shape[0] // 2
    return shift(one[:half], axis, 1), shift(three[half:], axis, 3)


def rolled(value, axis, by):
    return lax.dynamic_slice_in_dim(jnp.concatenate([value, value], axis), by, 4, axis)


def dot(a, b, da, db):
    return lax.dot_general(a, b, (((da,), (db,)), ((), ())), preferred_element_type=F32)


def thirds(value):
    one = lax.reduce_precision(value, 8, 7)
    two = lax.reduce_precision(value - one, 8, 7)
    three = lax.reduce_precision(value - one - two, 8, 7)
    return jnp.concatenate([one, two, three]).astype(BF)


sync = lambda *values: lax.optimization_barrier(values)
cat = lambda *values: jnp.concatenate(values, 0)


def params(limit=60):
    return pltpu.CompilerParams(dimension_semantics=("arbitrary",), vmem_limit_bytes=limit << 20)


def fetch(pieces, tokens_ref, sems):
    copies, at = [], 0
    for i, piece in enumerate(pieces):
        size = piece.shape[0]
        copies.append(pltpu.make_async_copy(piece, tokens_ref.at[pl.ds(at, size)], sems.at[i]))
        copies[-1].start()
        at += size
    return copies


def part_kernel(count, at, *refs):
    pieces, weight_ref, (part_ref, tokens_ref, staged_ref, sems, out_sem) = refs[:count], refs[count], refs[-5:]
    for copy in fetch(pieces, tokens_ref, sems):
        copy.wait()
    part = dot(tokens_ref[...], weight_ref[...], 1, 1)
    staged_ref[...] = part.reshape(16, 8, 8, 512).swapaxes(0, 1).astype(BF)
    copy = pltpu.make_async_copy(staged_ref, part_ref.at[:, pl.ds(at, 16)], out_sem)
    copy.start()
    copy.wait()


def grad_kernel(*refs):
    pieces, (feats_ref, grad_ref, grad_other_ref, tokens_ref, sems) = refs[:6], refs[6:]
    copies = fetch(pieces, tokens_ref, sems)
    feats = [feats_ref[:, i].astype(F32).swapaxes(0, 1).reshape(1024, 512).astype(BF) for i in range(2)]
    for copy in copies:
        copy.wait()
    grad = dot(jnp.concatenate(feats, 0), tokens_ref[...], 0, 0)
    grad_ref[...] = grad[:256]
    grad_other_ref[...] = grad[256:].astype(BF)


def place_kernel(places_ref, got_ref, out_ref):
    for i in range(16):
        out_ref[places_ref[i], :8] = jnp.sum(got_ref[:, 16 + i].astype(F32), 0)
        out_ref[i, 8:] = jnp.sum(got_ref[:, i].astype(F32), 0)


def last_kernel(
    grad_ref, other_ref, one_ref, two_ref, master_ref, new_one_ref, new_two_ref, direction_ref, sums_ref, acc_ref
):
    step = pl.program_id(0)

    @pl.when(step == 0)
    def _():
        acc_ref[...] = jnp.zeros_like(acc_ref)

    grad = grad_ref[...] + other_ref[...].astype(F32)
    master = master_ref[...]
    new_one = beta_one * one_ref[...] + (1.0 - beta_one) * grad
    new_two = beta_two * two_ref[...] + (1.0 - beta_two) * grad * grad
    direction = new_one / corr_one / (jnp.sqrt(new_two / corr_two) + adam_eps) + decay * master
    new_one_ref[...] = new_one
    new_two_ref[...] = new_two
    direction_ref[...] = direction
    fold = lambda value: jnp.sum((value * value).reshape(-1, 8, 1792), 0)
    acc_ref[0] += fold(master)
    acc_ref[1] += fold(direction)

    @pl.when(step == pl.num_programs(0) - 1)
    def _():
        lane = lax.broadcasted_iota(jnp.int32, sums_ref.shape, 1)
        sums_ref[...] = jnp.where(
            lane == 0, jnp.sum(acc_ref[0]), jnp.where(lane == 1, jnp.sum(acc_ref[1]), 0.0)
        )


def whole(*shape):
    return pl.BlockSpec(shape, lambda i: (0,) * len(shape))


def cost(flops, size):
    return pl.CostEstimate(flops=flops, bytes_accessed=size, transcendentals=0)


def on_device(activations, hidden_grad, master, moment_one, moment_two):
    zh, y, c = (lax.axis_index(n) for n in DP)
    f32 = jax.ShapeDtypeStruct((256, 1792), F32)

    halves = hidden_grad.reshape(8, 2, 8, 1792)
    second = lax.all_gather(halves[:, 1].reshape(64, 1792), CH, axis=0, tiled=True)
    mine = halves[:, 0].reshape(64, 1792)

    z1, z3 = ends(mine, "zh")
    rows = lax.all_to_all(activations, TP, split_axis=0, concat_axis=1, tiled=True)
    z1, z3, rows, master_late = sync(z1, z3, rows, master)
    z2 = middle(z1, z3, "zh")
    rows = lax.all_to_all(rows, CH, split_axis=1, concat_axis=0, tiled=True)
    *z2, rows = sync(*z2, rows)

    y0 = cat(mine, z1, *z2, z3)
    y1, y3 = ends(y0, "y")
    rows = lax.dynamic_slice_in_dim(jnp.concatenate([rows, rows[:, :256]], 1), 256 * c, 512, 1)
    rows = rows.reshape(4, 4, 2, 8, 512).transpose(2, 1, 0, 3, 4)
    rows = jnp.stack([rows[1].swapaxes(0, 1), rolled(rolled(rows[0], 0, y), 1, zh)])
    copies = jnp.broadcast_to(rows.reshape(1, 2, 16, 8, 512), (8, 2, 16, 8, 512))
    feats = lax.all_to_all(copies, TP, split_axis=0, concat_axis=0, tiled=True)
    y2 = middle(y1, y3, "y")

    weight = master_late.astype(BF)
    weight_other = shift(weight, "c", 1, 2)
    both = jnp.where(c == 0, cat(weight, weight_other), cat(weight_other, weight))
    both, second = sync(both, second)

    vmem, hbm = (pl.BlockSpec(memory_space=space) for space in (pltpu.VMEM, pltpu.HBM))
    limit = pltpu.CompilerParams(vmem_limit_bytes=60 << 20)

    def partials(pieces, at, *buffer):
        count = len(pieces)
        return pl.pallas_call(
            functools.partial(part_kernel, count, at),
            in_specs=[hbm] * count + [vmem] + [hbm] * len(buffer),
            out_specs=hbm,
            out_shape=jax.ShapeDtypeStruct((8, 32, 8, 512), BF),
            input_output_aliases={count + 1: 0} if buffer else {},
            scratch_shapes=[
                pltpu.VMEM((1024, 1792), BF),
                pltpu.VMEM((8, 16, 8, 512), BF),
                pltpu.SemaphoreType.DMA((count,)),
                pltpu.SemaphoreType.DMA,
            ],
            compiler_params=limit,
            cost_estimate=cost(2 * 1024 * 512 * 1792, 8 << 20),
        )(*pieces, both, *buffer)

    part = partials([second], 0)
    *y2, y0, y1, y3, second, part = sync(*y2, y0, y1, y3, second, part)
    part = partials([y0, y1, *y2, y3], 16, part)
    pieces = (second, y0, y1, *y2, y3)
    got = lax.all_to_all(part, TP, split_axis=0, concat_axis=0, tiled=True)
    feats, _ = sync(feats, part)
    grad, grad_other = pl.pallas_call(
        grad_kernel,
        in_specs=[hbm] * 6 + [vmem],
        out_specs=[vmem] * 2,
        out_shape=[f32, jax.ShapeDtypeStruct((256, 1792), BF)],
        scratch_shapes=[pltpu.VMEM((2048, 1792), BF), pltpu.SemaphoreType.DMA((6,))],
        compiler_params=limit,
        cost_estimate=cost(2 * 2048 * 512 * 1792, 12 << 20),
    )(*pieces, feats)
    grad_other = shift(grad_other, "c", 1, 2)
    places = jnp.stack([4 * ((zh + z) % 4) + (y + k) % 4 for k in range(4) for z in range(4)])
    out = pl.pallas_call(
        place_kernel,
        out_shape=jax.ShapeDtypeStruct((16, 16, 512), F32),
        in_specs=[pl.BlockSpec(memory_space=pltpu.SMEM)] + [pl.BlockSpec(memory_space=pltpu.VMEM)],
        compiler_params=pltpu.CompilerParams(vmem_limit_bytes=8 << 20),
        cost_estimate=cost(0, 2 << 20),
    )(places.astype(jnp.int32), got)
    slab = pl.BlockSpec((128, 1792), lambda i: (i, 0))
    new_one, new_two, direction, sums = pl.pallas_call(
        last_kernel,
        grid=(2,),
        in_specs=[slab] * 5,
        out_specs=[slab] * 3 + [whole(16, 128)],
        out_shape=[f32] * 3 + [jax.ShapeDtypeStruct((16, 128), F32)],
        scratch_shapes=[pltpu.VMEM((2, 8, 1792), F32)],
        compiler_params=params(),
        cost_estimate=cost(0, 8 << 20),
    )(grad, grad_other, moment_one, moment_two, master)
    sums, out = sync(sums, out)
    sums = jnp.sum(lax.all_to_all(sums, ("c",) + TP, split_axis=0, concat_axis=0, tiled=True), 0)[:2]

    extra = jnp.broadcast_to(jnp.pad(thirds(sums), (0, 506)), (16, 8, 512))
    out = jnp.concatenate([out.astype(BF), extra], 1)
    out = lax.all_to_all(out, CH, split_axis=0, concat_axis=0, tiled=True)
    input_grad = out[:, :16].transpose(1, 0, 2).reshape(16, 8192)
    sums = jnp.sum(out[:, 16, :6].astype(F32).reshape(16, 3, 2), (0, 1))
    trust = jnp.sqrt(sums[0]) / (jnp.sqrt(sums[1]) + adam_eps)
    return (input_grad, trust * direction, new_one, new_two)


def solution(mesh):
    fine = Mesh(mesh.devices.reshape(4, 4, 2, 2, 4), DP + TP)
    return jax.shard_map(
        on_device,
        mesh=fine,
        in_specs=(P(DP, TP),) * 5,
        out_specs=(P(DP + TP, None), P(DP, TP), P(DP, TP), P(DP, TP)),
        check_vma=False,
    )
```
